32 devices in a mesh: ctx: 16 (over z, y, core), hg: 2 (over x).
Axes of the slice: x: 2, y: 2, z: 4, core: 2. Of those that a mesh axis runs over, the one named last changes fastest.
Arguments:
- query_latent_plain: bfloat16 [2048, 32, 512], P('ctx', 'hg'), may hold values from -40 to 40
- query_rope: bfloat16 [2048, 32, 64], P('ctx', 'hg'), may hold values from -40 to 40
- latent_nope: bfloat16 [2048, 512], P('ctx'), may hold values from -6 to 6
- latent_rope: bfloat16 [2048, 64], P('ctx'), may hold values from -6 to 6
- latent_output_gradient: bfloat16 [2048, 32, 512], P('ctx', 'hg'), may hold values from -5 to 5
- block_mask: int32 [32, 32], replicated, may hold values from 0 to 1, as said below
Outputs:
- d_query_nope: bfloat16 [2048, 32, 512], P('ctx', 'hg')
- d_query_rope: bfloat16 [2048, 32, 64], P('ctx', 'hg')
- d_latent_nope: float32 [2048, 512], P(('ctx', 'hg'))
- d_latent_rope: float32 [2048, 64], P(('ctx', 'hg'))
The draws below stay inside these ranges and needn't reach their ends.
Inputs may be any that keep to these rules, and one draw needn't show every extreme that they name: Every mask block may attend to itself: block_mask[b, b] = 1.
All inputs are finite; a program needn't handle non-finite values.
Results may differ from the reference program's by a relative error of at most 0.012.
Values may be sent and summed in bfloat16 or wider, within the bound.
A program may use at most 64 MiB of HBM per device.

```python
import jax
import jax.numpy as jnp
from jax import lax

LATENT_WIDTH = 512
ROTARY_WIDTH = 64
QUERY_PER_SLOT = 128
WINDOW = 4
HEAD_COUNT = 32
TOKEN_COUNT = 2048
BLK = 64
BLOCKS = 32
N_CTX = 16


def latent_pair(key):
    drawn_part = jax.random.truncated_normal(jax.random.fold_in(key, 11), -4.0, 4.0, (TOKEN_COUNT, LATENT_WIDTH), jnp.float32)
    rope = jax.random.truncated_normal(jax.random.fold_in(key, 12), -4.0, 4.0, (TOKEN_COUNT, ROTARY_WIDTH), jnp.float32)
    return (drawn_part, rope)


def draw_latent_nope(key, part):
    return latent_pair(key)[0].astype(jnp.bfloat16)


def draw_latent_rope(key, part):
    return latent_pair(key)[1].astype(jnp.bfloat16)


def draw_query_latent_plain(key, part):
    base_offset = jax.random.truncated_normal(jax.random.fold_in(key, 21), -4.0, 4.0, (TOKEN_COUNT, HEAD_COUNT, LATENT_WIDTH), jnp.float32)
    return base_offset.astype(jnp.bfloat16)


def draw_query_rope(key, part):
    base_offset = jax.random.truncated_normal(jax.random.fold_in(key, 22), -4.0, 4.0, (TOKEN_COUNT, HEAD_COUNT, ROTARY_WIDTH), jnp.float32)
    return base_offset.astype(jnp.bfloat16)


def draw_block_mask(key, part):
    order = jax.random.permutation(jax.random.fold_in(key, 41), N_CTX).astype(jnp.int32)
    blocks = jnp.arange(BLOCKS, dtype=jnp.int32)
    owner = order[blocks // 2]
    place = jnp.where(blocks % 2 == 0, owner, 2 * N_CTX - 1 - owner)
    keep = jax.random.randint(jax.random.fold_in(key, 42), (BLOCKS, BLOCKS), 0, 4) > 0
    earlier = place[None, :] <= place[:, None]
    same = place[None, :] == place[:, None]
    return (earlier & (keep | same)).astype(jnp.int32)


def shard_levels(key, dims, shards, smallest, high):
    def one(axis_at, shards_of):
        steps = jax.random.uniform(jax.random.fold_in(jax.random.fold_in(key, 6), axis_at), (shards_of,), jnp.float32, smallest / len(shards), high / len(shards))
        return jnp.repeat(jnp.exp(steps), dims[axis_at] // shards_of).reshape((-1,) + (1,) * (len(dims) - axis_at - 1))

    loudness = one(*shards[0])
    for cut in shards[1:]:
        loudness = loudness * one(*cut)
    return loudness


def normal_values(rng, shape, spread, limit, cuts=(), held_as=jnp.bfloat16):
    values = spread * jax.random.normal(rng, shape, jnp.float32)
    if cuts:
        values = values * shard_levels(rng, shape, cuts, -0.22, 0.18)
    return jnp.clip(values, -limit, limit).astype(held_as)


def setup_inputs(seed: int = 0) -> dict:
    splits = jax.random.split(jax.random.key(seed), 7)
    query_latent_plain = draw_query_latent_plain(jax.random.fold_in(splits[6], 71), 0)
    query_rope = draw_query_rope(jax.random.fold_in(splits[6], 71), 0)
    latent_nope = draw_latent_nope(jax.random.fold_in(splits[6], 71), 0)
    latent_rope = draw_latent_rope(jax.random.fold_in(splits[6], 71), 0)
    latent_output_gradient = normal_values(splits[4], (TOKEN_COUNT, HEAD_COUNT, LATENT_WIDTH), 1.0, 5.0, ((0, 16), (1, 2)))
    block_mask = draw_block_mask(jax.random.fold_in(splits[6], 71), 0)
    return {"query_latent_plain": query_latent_plain, "query_rope": query_rope, "latent_nope": latent_nope, "latent_rope": latent_rope, "latent_output_gradient": latent_output_gradient, "block_mask": block_mask}


SCORE_SCALE = 192.0 ** -0.5


def reference(query_latent_plain, query_rope, latent_nope, latent_rope, latent_output_gradient, block_mask):
    row_count = QUERY_PER_SLOT * HEAD_COUNT

    def one_cycle(carry, cycle):
        plain_gradient, rotary_gradient = carry
        start_index = cycle * QUERY_PER_SLOT
        query_plain = lax.dynamic_slice_in_dim(query_latent_plain, start_index, QUERY_PER_SLOT, 0).reshape(row_count, LATENT_WIDTH)
        q_rope = lax.dynamic_slice_in_dim(query_rope, start_index, QUERY_PER_SLOT, 0).reshape(row_count, ROTARY_WIDTH)
        output_gradient_rows = lax.dynamic_slice_in_dim(latent_output_gradient, start_index, QUERY_PER_SLOT, 0).reshape(row_count, LATENT_WIDTH)
        sources = (cycle - jnp.arange(WINDOW, dtype=jnp.int32)) % N_CTX
        key_tokens = (sources[:, None] * QUERY_PER_SLOT + jnp.arange(QUERY_PER_SLOT, dtype=jnp.int32)[None, :]).reshape(-1)
        k_nope = latent_nope[key_tokens]
        k_rope = latent_rope[key_tokens]
        row_block = 2 * cycle + (jnp.arange(row_count, dtype=jnp.int32) // HEAD_COUNT) // BLK
        key_block = (2 * sources[:, None] + jnp.arange(QUERY_PER_SLOT, dtype=jnp.int32)[None, :] // BLK).reshape(-1)
        allowed = block_mask[row_block][:, key_block] == 1
        scores = (jnp.dot(query_plain, k_nope.T, preferred_element_type=jnp.float32)
                  + jnp.dot(q_rope, k_rope.T, preferred_element_type=jnp.float32)) * SCORE_SCALE
        masked = jnp.where(allowed, scores, -jnp.inf)
        top = jnp.max(masked, axis=1)
        lse = top + jnp.log(jnp.sum(jnp.exp(masked - top[:, None]), axis=1))
        prob = jnp.exp(masked - lse[:, None])
        dprob = jnp.dot(output_gradient_rows, k_nope.T, preferred_element_type=jnp.float32)
        delta = jnp.sum(prob * dprob, axis=1)
        dscore = (prob * (dprob - delta[:, None])).astype(jnp.bfloat16)
        prob_low = prob.astype(jnp.bfloat16)
        query_plain_gradient = (SCORE_SCALE * jnp.dot(dscore, k_nope, preferred_element_type=jnp.float32)).astype(jnp.bfloat16)
        query_rotary_gradient = (SCORE_SCALE * jnp.dot(dscore, k_rope, preferred_element_type=jnp.float32)).astype(jnp.bfloat16)
        dk_nope = SCORE_SCALE * jnp.dot(dscore.T, query_plain, preferred_element_type=jnp.float32) + jnp.dot(prob_low.T, output_gradient_rows, preferred_element_type=jnp.float32)
        dk_rope = SCORE_SCALE * jnp.dot(dscore.T, q_rope, preferred_element_type=jnp.float32)
        plain_gradient = plain_gradient.at[key_tokens].add(dk_nope)
        rotary_gradient = rotary_gradient.at[key_tokens].add(dk_rope)
        return (plain_gradient, rotary_gradient), (query_plain_gradient.reshape(QUERY_PER_SLOT, HEAD_COUNT, LATENT_WIDTH), query_rotary_gradient.reshape(QUERY_PER_SLOT, HEAD_COUNT, ROTARY_WIDTH))

    initial_state = (jnp.zeros((TOKEN_COUNT, LATENT_WIDTH), jnp.float32), jnp.zeros((TOKEN_COUNT, ROTARY_WIDTH), jnp.float32))
    (plain_gradient, rotary_gradient), (query_plain_gradient, query_rotary_gradient) = lax.scan(one_cycle, initial_state, jnp.arange(N_CTX, dtype=jnp.int32))
    return (query_plain_gradient.reshape(TOKEN_COUNT, HEAD_COUNT, LATENT_WIDTH), query_rotary_gradient.reshape(TOKEN_COUNT, HEAD_COUNT, ROTARY_WIDTH), plain_gradient, rotary_gradient)
```

```python
import functools
import math

import jax
import jax.numpy as jnp
from jax import lax
from jax.experimental import pallas as pl
from jax.experimental.pallas import tpu as pltpu
from jax.sharding import PartitionSpec as P

WINDOW = 4
PAIRS = WINDOW // 2
SCORE_SCALE = 192.0 ** (-0.5)
LOG2E = math.log2(math.e)
LANES = 128
MESH = pl.DeviceIdType.MESH


def dot_nt(a, b):
    return lax.dot_general(a, b, (((1,), (1,)), ((), ())), preferred_element_type=jnp.float32)


def dot_tn(a, b):
    return lax.dot_general(a, b, (((0,), (0,)), ((), ())), preferred_element_type=jnp.float32)


def kernel(
    n_ctx,
    n_hg,
    mask_ref,
    q_hbm,
    qr_hbm,
    kn_hbm,
    kr_hbm,
    g_hbm,
    dq_ref,
    dqr_ref,
    dkn_ref,
    dkr_ref,
    q_ref,
    qr_ref,
    g_ref,
    kr_own,
    kcat,
    x_ref,
    dp_ref,
    prob_ref,
    ds_ref,
    bias_ref,
    acc_ref,
    dk_out,
    dk_in,
    load_sem,
    k_send,
    k_recv,
    d_send,
    d_recv,
):
    rows, latent = q_ref.shape
    rope = qr_ref.shape[1]
    keys = kcat.shape[1]
    piece = keys // n_hg
    pair = 2 * keys
    blocks = mask_ref.shape[0] // n_ctx
    block_rows = rows // blocks
    tile = 256
    tiles = rows // tile
    c = lax.axis_index("ctx")
    h = lax.axis_index("hg")

    load_kn = pltpu.make_async_copy(kn_hbm, kcat.at[0, :, pl.ds(0, latent)], load_sem.at[0])
    load_kr = pltpu.make_async_copy(kr_hbm, kr_own, load_sem.at[1])
    load_q = pltpu.make_async_copy(q_hbm, q_ref, load_sem.at[2])
    load_qr = pltpu.make_async_copy(qr_hbm, qr_ref, load_sem.at[3])
    load_g = pltpu.make_async_copy(g_hbm, g_ref, load_sem.at[4])
    load_kn.start()
    load_kr.start()

    barrier = pltpu.get_barrier_semaphore()
    greeted = 0
    for d in range(1 - WINDOW, WINDOW):
        for k in range(n_hg):
            if d == 0 and k == 0:
                continue
            pl.semaphore_signal(
                barrier,
                inc=1,
                device_id=(lax.rem(c + d + n_ctx, n_ctx), lax.rem(h + k, n_hg)),
                device_id_type=MESH,
            )
            greeted += 1
    load_q.start()
    load_qr.start()
    load_g.start()

    load_kn.wait()
    load_kr.wait()
    kcat[0, :, latent:] = jnp.zeros((keys, kcat.shape[2] - latent), kcat.dtype)
    kcat[0, :, latent : latent + rope] = kr_own[...]
    pl.semaphore_wait(barrier, greeted)

    sends = []
    for d in range(1, WINDOW):
        copy = pltpu.make_async_remote_copy(
            src_ref=kcat.at[0],
            dst_ref=kcat.at[d],
            send_sem=k_send.at[d],
            recv_sem=k_recv.at[d],
            device_id=(lax.rem(c + d, n_ctx), h),
            device_id_type=MESH,
        )
        copy.start()
        sends.append(copy)

    key_block = lax.broadcasted_iota(jnp.int32, (1, WINDOW * keys), 1) // (keys // blocks)
    for rb in range(blocks):
        bias = jnp.zeros((1, WINDOW * keys), jnp.float32)
        for d in range(WINDOW):
            source = lax.rem(c - d + n_ctx, n_ctx)
            for kb in range(blocks):
                bit = mask_ref[c * blocks + rb, source * blocks + kb]
                value = jnp.where(bit == 1, 0.0, -jnp.inf).astype(jnp.float32)
                bias = jnp.where(key_block == d * blocks + kb, value, bias)
        bias_ref[rb : rb + 1, :] = bias

    acc_ref[...] = jnp.zeros_like(acc_ref)
    load_q.wait()
    load_qr.wait()
    load_g.wait()

    for p in range(PAIRS):
        for d in (2 * p, 2 * p + 1):
            if d > 0:
                sends[d - 1].wait_recv()
        cols = slice(p * pair, (p + 1) * pair)

        def score_tile(i, _, p=p, cols=cols):
            r = pl.ds(pl.multiple_of(i * tile, tile), tile)
            kn = kcat[2 * p : 2 * p + 2, :, :latent].reshape(pair, latent)
            kr = kcat[2 * p : 2 * p + 2, :, latent : latent + rope].reshape(pair, rope)
            bias = bias_ref[pl.ds(i * tile // block_rows, 1), cols]
            s = dot_nt(q_ref[r, :], kn) + dot_nt(qr_ref[r, :], kr)
            x_ref[r, cols] = s * (SCORE_SCALE * LOG2E) + bias
            dp_ref[r, cols] = dot_nt(g_ref[r, :], kn)
            return 0

        lax.fori_loop(0, tiles, score_tile, 0)

    def add_key_grads(p, r, ds, prob):
        q = q_ref[r, :]
        acc_ref[p, :, :latent] += dot_tn(ds, q) + dot_tn(prob, g_ref[r, :])
        acc_ref[p, :, latent : latent + rope] += dot_tn(ds, qr_ref[r, :])

    def send_key_grads(p):
        out = []
        for d in (2 * p + 1, 2 * p):
            block = acc_ref[p, (d - 2 * p) * keys : (d - 2 * p + 1) * keys, :]
            dk_out[d] = block.reshape(n_hg, piece, block.shape[1]).astype(dk_out.dtype)
            for k in reversed(range(n_hg)):
                if d == 0 and k == 0:
                    continue
                peer = lax.rem(h + k, n_hg)
                copy = pltpu.make_async_remote_copy(
                    src_ref=dk_out.at[d, peer],
                    dst_ref=dk_in.at[d, k],
                    send_sem=d_send.at[d, k],
                    recv_sem=d_recv.at[d, k],
                    device_id=(lax.rem(c - d + n_ctx, n_ctx), peer),
                    device_id_type=MESH,
                )
                copy.start()
                out.append((d, k, copy))
        return out

    last = PAIRS - 1

    def soft_tile(i, _):
        r = pl.ds(pl.multiple_of(i * tile, tile), tile)
        x = x_ref[r, :]
        dp = dp_ref[r, :]
        e = jnp.exp2(x - jnp.max(x, axis=1, keepdims=True))
        inv = 1.0 / jnp.sum(e, axis=1, keepdims=True)
        delta = jnp.sum(e * dp, axis=1, keepdims=True) * inv
        prob = (e * inv).astype(jnp.bfloat16)
        ds = (e * (inv * SCORE_SCALE) * (dp - delta)).astype(jnp.bfloat16)
        prob_ref[r, :] = prob
        ds_ref[r, :] = ds
        add_key_grads(last, r, ds[:, last * pair :], prob[:, last * pair :])
        return 0

    lax.fori_loop(0, tiles, soft_tile, 0)
    moving = send_key_grads(last)

    for p in reversed(range(last)):
        cols = slice(p * pair, (p + 1) * pair)

        def grad_tile(i, _, p=p, cols=cols):
            r = pl.ds(pl.multiple_of(i * tile, tile), tile)
            add_key_grads(p, r, ds_ref[r, cols], prob_ref[r, cols])
            return 0

        lax.fori_loop(0, tiles, grad_tile, 0)
        moving += send_key_grads(p)

    def query_tile(i, _):
        r = pl.ds(pl.multiple_of(i * tile, tile), tile)
        ds = ds_ref[r, :]
        kn = kcat[:, :, :latent].reshape(WINDOW * keys, latent)
        kr = kcat[:, :, latent : latent + rope].reshape(WINDOW * keys, rope)
        dq_ref[r, :] = jnp.dot(ds, kn, preferred_element_type=jnp.float32).astype(dq_ref.dtype)
        dqr_ref[r, :] = jnp.dot(ds, kr, preferred_element_type=jnp.float32).astype(dqr_ref.dtype)
        return 0

    lax.fori_loop(0, tiles, query_tile, 0)

    total = acc_ref[0, pl.ds(pl.multiple_of(h * piece, piece), piece), :]
    for d, k, copy in sorted(moving, key=lambda m: (-m[0], m[1])):
        copy.wait_recv()
        total = total + dk_in[d, k].astype(jnp.float32)
    dkn_ref[...] = total[:, :latent]
    dkr_ref[...] = total[:, latent : latent + rope]

    for copy in sends:
        copy.wait_send()
    for _, _, copy in moving:
        copy.wait_send()


def on_device(n_ctx, n_hg, q, qr, kn, kr, g, block_mask):
    tokens, heads, latent = q.shape
    rope = qr.shape[2]
    rows = tokens * heads
    width = -(-(latent + rope) // LANES) * LANES
    piece = tokens // n_hg
    blocks = block_mask.shape[0] // n_ctx
    bf16, f32 = jnp.bfloat16, jnp.float32
    hbm = pl.BlockSpec(memory_space=pl.ANY)
    vmem = pl.BlockSpec(memory_space=pltpu.VMEM)
    dq, dqr, dkn, dkr = pl.pallas_call(
        functools.partial(kernel, n_ctx, n_hg),
        out_shape=(
            jax.ShapeDtypeStruct((rows, latent), bf16),
            jax.ShapeDtypeStruct((rows, rope), bf16),
            jax.ShapeDtypeStruct((piece, latent), f32),
            jax.ShapeDtypeStruct((piece, rope), f32),
        ),
        in_specs=[pl.BlockSpec(memory_space=pltpu.SMEM)] + [hbm] * 5,
        out_specs=[vmem] * 4,
        scratch_shapes=[
            pltpu.VMEM((rows, latent), bf16),
            pltpu.VMEM((rows, rope), bf16),
            pltpu.VMEM((rows, latent), bf16),
            pltpu.VMEM((tokens, rope), bf16),
            pltpu.VMEM((WINDOW, tokens, width), bf16),
            pltpu.VMEM((rows, WINDOW * tokens), f32),
            pltpu.VMEM((rows, WINDOW * tokens), f32),
            pltpu.VMEM((rows, WINDOW * tokens), bf16),
            pltpu.VMEM((rows, WINDOW * tokens), bf16),
            pltpu.VMEM((blocks, WINDOW * tokens), f32),
            pltpu.VMEM((PAIRS, 2 * tokens, width), f32),
            pltpu.VMEM((WINDOW, n_hg, piece, width), bf16),
            pltpu.VMEM((WINDOW, n_hg, piece, width), bf16),
            pltpu.SemaphoreType.DMA((5,)),
            pltpu.SemaphoreType.DMA((WINDOW,)),
            pltpu.SemaphoreType.DMA((WINDOW,)),
            pltpu.SemaphoreType.DMA((WINDOW, n_hg)),
            pltpu.SemaphoreType.DMA((WINDOW, n_hg)),
        ],
        compiler_params=pltpu.CompilerParams(
            collective_id=0, has_side_effects=True, vmem_limit_bytes=44 * 1024 * 1024
        ),
    )(block_mask, q.reshape(rows, latent), qr.reshape(rows, rope), kn, kr, g.reshape(rows, latent))
    return dq.reshape(tokens, heads, latent), dqr.reshape(tokens, heads, rope), dkn, dkr


def solution(mesh):
    wide = P("ctx", "hg", None)
    owned = P(("ctx", "hg"), None)
    return jax.shard_map(
        functools.partial(on_device, mesh.shape["ctx"], mesh.shape["hg"]),
        mesh=mesh,
        in_specs=(wide, wide, P("ctx", None), P("ctx", None), wide, P()),
        out_specs=(wide, wide, owned, owned),
        check_vma=False,
    )
```

```python
import functools
import math

import jax
import jax.numpy as jnp
from jax import lax
from jax.experimental import pallas as pl
from jax.experimental.pallas import tpu as pltpu
from jax.sharding import PartitionSpec as P

WINDOW = 4
PAIRS = WINDOW // 2
SCORE_SCALE = 192.0 ** (-0.5)
LOG2E = math.log2(math.e)
LANES = 128
MESH = pl.DeviceIdType.MESH


def dot_nn(a, b):
    return jnp.dot(a, b, preferred_element_type=jnp.float32)


def dot_nt(a, b):
    return lax.dot_general(a, b, (((1,), (1,)), ((), ())), preferred_element_type=jnp.float32)


def dot_tn(a, b):
    return lax.dot_general(a, b, (((0,), (0,)), ((), ())), preferred_element_type=jnp.float32)


def kernel(
    n_ctx,
    n_hg,
    mask_ref,
    q_hbm,
    qr_hbm,
    kn_hbm,
    kr_hbm,
    g_hbm,
    dq_ref,
    dqr_ref,
    dkn_ref,
    dkr_ref,
    q_ref,
    qrt_ref,
    qr_wide,
    qr_ref,
    g_ref,
    kn_all,
    krt_all,
    dq_tile,
    dqr_wide,
    dqrt_ref,
    x_ref,
    dp_ref,
    prob_ref,
    ds_ref,
    bias_ref,
    acc_ref,
    dk_out,
    dk_in,
    load_sem,
    store_sem,
    k_send,
    k_recv,
    d_send,
    d_recv,
):
    rows, latent = q_ref.shape
    rope = qr_ref.shape[1]
    heads = qrt_ref.shape[0]
    tokens = qrt_ref.shape[2]
    keys = kn_all.shape[1]
    piece = keys // n_hg
    pair = 2 * keys
    blocks = mask_ref.shape[0] // n_ctx
    block_rows = rows // blocks
    tile = 512
    tiles = rows // tile
    soft_rows = 256
    sub_rows = 32
    c = lax.axis_index("ctx")
    h = lax.axis_index("hg")

    load_kn = pltpu.make_async_copy(kn_hbm, kn_all.at[0], load_sem.at[0])
    load_kr = pltpu.make_async_copy(kr_hbm, krt_all.at[0], load_sem.at[1])
    load_q = pltpu.make_async_copy(q_hbm, q_ref, load_sem.at[2])
    load_qr = pltpu.make_async_copy(qr_hbm, qrt_ref, load_sem.at[3])
    load_g = pltpu.make_async_copy(g_hbm, g_ref, load_sem.at[4])
    load_kn.start()
    load_kr.start()

    barrier = pltpu.get_barrier_semaphore()
    greeted = 0
    for d in range(1 - WINDOW, WINDOW):
        for k in range(n_hg):
            if d == 0 and k == 0:
                continue
            pl.semaphore_signal(
                barrier,
                inc=1,
                device_id=(lax.rem(c + d + n_ctx, n_ctx), lax.rem(h + k, n_hg)),
                device_id_type=MESH,
            )
            greeted += 1
    load_q.start()
    load_qr.start()
    load_g.start()

    load_kn.wait()
    load_kr.wait()
    pl.semaphore_wait(barrier, greeted)

    sends = []
    for d in range(1, WINDOW):
        both = []
        for part, buffer in enumerate((kn_all, krt_all)):
            copy = pltpu.make_async_remote_copy(
                src_ref=buffer.at[0],
                dst_ref=buffer.at[d],
                send_sem=k_send.at[d, part],
                recv_sem=k_recv.at[d, part],
                device_id=(lax.rem(c + d, n_ctx), h),
                device_id_type=MESH,
            )
            copy.start()
            both.append(copy)
        sends.append(both)

    key_block = lax.broadcasted_iota(jnp.int32, (1, WINDOW * keys), 1) // (keys // blocks)
    for rb in range(blocks):
        bias = jnp.zeros((1, WINDOW * keys), jnp.float32)
        for d in range(WINDOW):
            source = lax.rem(c - d + n_ctx, n_ctx)
            for kb in range(blocks):
                bit = mask_ref[c * blocks + rb, source * blocks + kb]
                value = jnp.where(bit == 1, 0.0, -jnp.inf).astype(jnp.float32)
                bias = jnp.where(key_block == d * blocks + kb, value, bias)
        bias_ref[rb : rb + 1, :] = bias

    acc_ref[...] = jnp.zeros_like(acc_ref)
    load_qr.wait()
    for head in range(heads):
        turned = qrt_ref[head].astype(jnp.float32).T
        qr_wide[pl.ds(head, tokens, stride=heads), :] = turned
    qr_ref[...] = qr_wide[...].astype(qr_ref.dtype)
    load_q.wait()
    load_g.wait()

    for p in range(PAIRS):
        for d in (2 * p, 2 * p + 1):
            if d > 0:
                for copy in sends[d - 1]:
                    copy.wait_recv()
        cols = slice(p * pair, (p + 1) * pair)

        def score_tile(i, _, p=p, cols=cols):
            r = pl.ds(pl.multiple_of(i * tile, tile), tile)
            kn = kn_all[2 * p : 2 * p + 2].reshape(pair, latent)
            krt = jnp.concatenate([krt_all[2 * p], krt_all[2 * p + 1]], axis=1)
            bias = bias_ref[pl.ds(i * tile // block_rows, 1), cols]
            s = dot_nt(q_ref[r, :], kn) + dot_nn(qr_ref[r, :], krt)
            x_ref[r, cols] = s * (SCORE_SCALE * LOG2E) + bias
            dp_ref[r, cols] = dot_nt(g_ref[r, :], kn)
            return 0

        lax.fori_loop(0, tiles, score_tile, 0)

    def add_key_grads(p, r, ds, prob):
        q = q_ref[r, :]
        acc_ref[p, :, :latent] += dot_tn(ds, q) + dot_tn(prob, g_ref[r, :])
        acc_ref[p, :, latent : latent + rope] += dot_tn(ds, qr_ref[r, :])

    def send_key_grads(p):
        out = []
        for d in (2 * p + 1, 2 * p):
            block = acc_ref[p, (d - 2 * p) * keys : (d - 2 * p + 1) * keys, :]
            dk_out[d] = block.reshape(n_hg, piece, block.shape[1]).astype(dk_out.dtype)
            for k in reversed(range(n_hg)):
                if d == 0 and k == 0:
                    continue
                peer = lax.rem(h + k, n_hg)
                copy = pltpu.make_async_remote_copy(
                    src_ref=dk_out.at[d, peer],
                    dst_ref=dk_in.at[d, k],
                    send_sem=d_send.at[d, k],
                    recv_sem=d_recv.at[d, k],
                    device_id=(lax.rem(c - d + n_ctx, n_ctx), peer),
                    device_id_type=MESH,
                )
                copy.start()
                out.append((d, k, copy))
        return out

    last = PAIRS - 1

    for start in range(0, rows, soft_rows):
        for at in range(start, start + soft_rows, sub_rows):
            r = slice(at, at + sub_rows)
            x = x_ref[r, :]
            dp = dp_ref[r, :]
            e = jnp.exp2(x - jnp.max(x, axis=1, keepdims=True))
            inv = 1.0 / jnp.sum(e, axis=1, keepdims=True)
            delta = jnp.sum(e * dp, axis=1, keepdims=True) * inv
            prob_ref[r, :] = (e * inv).astype(jnp.bfloat16)
            ds_ref[r, :] = (e * (inv * SCORE_SCALE) * (dp - delta)).astype(jnp.bfloat16)
        r = slice(start, start + soft_rows)
        cols = slice(last * pair, (last + 1) * pair)
        add_key_grads(last, r, ds_ref[r, cols], prob_ref[r, cols])
    moving = send_key_grads(last)

    for p in reversed(range(last)):
        cols = slice(p * pair, (p + 1) * pair)

        def grad_tile(i, _, p=p, cols=cols):
            r = pl.ds(pl.multiple_of(i * tile, tile), tile)
            add_key_grads(p, r, ds_ref[r, cols], prob_ref[r, cols])
            return 0

        lax.fori_loop(0, tiles, grad_tile, 0)
        moving += send_key_grads(p)

    stores = []
    for i in range(tiles):
        r = slice(i * tile, (i + 1) * tile)
        ds = ds_ref[r, :]
        kn = kn_all[...].reshape(WINDOW * keys, latent)
        krt = jnp.concatenate([krt_all[d] for d in range(WINDOW)], axis=1)
        dq_tile[r, :] = dot_nn(ds, kn).astype(dq_tile.dtype)
        dqr_wide[r, :] = dot_nt(ds, krt)
        copy = pltpu.make_async_copy(dq_tile.at[r, :], dq_ref.at[r, :], store_sem.at[i])
        copy.start()
        stores.append(copy)
    for head in range(heads):
        part = dqr_wide[pl.ds(head, tokens, stride=heads), :]
        dqrt_ref[head] = part.T.astype(dqrt_ref.dtype)
    copy = pltpu.make_async_copy(dqrt_ref, dqr_ref, store_sem.at[tiles])
    copy.start()
    stores.append(copy)

    total = acc_ref[0, pl.ds(pl.multiple_of(h * piece, piece), piece), :]
    for d, k, copy in sorted(moving, key=lambda m: (-m[0], m[1])):
        copy.wait_recv()
        total = total + dk_in[d, k].astype(jnp.float32)
    dkn_ref[...] = total[:, :latent]
    dkr_ref[...] = total[:, latent : latent + rope]

    for both in sends:
        for copy in both:
            copy.wait_send()
    for copy in stores:
        copy.wait()
    for _, _, copy in moving:
        copy.wait_send()


def on_device(n_ctx, n_hg, q, qr, kn, kr, g, block_mask):
    tokens, heads, latent = q.shape
    rope = qr.shape[2]
    rows = tokens * heads
    width = -(-(latent + rope) // LANES) * LANES
    piece = tokens // n_hg
    blocks = block_mask.shape[0] // n_ctx
    bf16, f32 = jnp.bfloat16, jnp.float32
    hbm = pl.BlockSpec(memory_space=pl.ANY)
    vmem = pl.BlockSpec(memory_space=pltpu.VMEM)
    dq, dqr, dkn, dkr = pl.pallas_call(
        functools.partial(kernel, n_ctx, n_hg),
        out_shape=(
            jax.ShapeDtypeStruct((rows, latent), bf16),
            jax.ShapeDtypeStruct((heads, rope, tokens), bf16),
            jax.ShapeDtypeStruct((piece, latent), f32),
            jax.ShapeDtypeStruct((piece, rope), f32),
        ),
        in_specs=[pl.BlockSpec(memory_space=pltpu.SMEM)] + [hbm] * 5,
        out_specs=[hbm, hbm, vmem, vmem],
        scratch_shapes=[
            pltpu.VMEM((rows, latent), bf16),
            pltpu.VMEM((heads, rope, tokens), bf16),
            pltpu.VMEM((rows, rope), f32),
            pltpu.VMEM((rows, rope), bf16),
            pltpu.VMEM((rows, latent), bf16),
            pltpu.VMEM((WINDOW, tokens, latent), bf16),
            pltpu.VMEM((WINDOW, rope, tokens), bf16),
            pltpu.VMEM((rows, latent), bf16),
            pltpu.VMEM((rows, rope), f32),
            pltpu.VMEM((heads, rope, tokens), bf16),
            pltpu.VMEM((rows, WINDOW * tokens), f32),
            pltpu.VMEM((rows, WINDOW * tokens), f32),
            pltpu.VMEM((rows, WINDOW * tokens), bf16),
            pltpu.VMEM((rows, WINDOW * tokens), bf16),
            pltpu.VMEM((blocks, WINDOW * tokens), f32),
            pltpu.VMEM((PAIRS, 2 * tokens, width), f32),
            pltpu.VMEM((WINDOW, n_hg, piece, width), bf16),
            pltpu.VMEM((WINDOW, n_hg, piece, width), bf16),
            pltpu.SemaphoreType.DMA((5,)),
            pltpu.SemaphoreType.DMA((rows // 512 + 1,)),
            pltpu.SemaphoreType.DMA((WINDOW, 2)),
            pltpu.SemaphoreType.DMA((WINDOW, 2)),
            pltpu.SemaphoreType.DMA((WINDOW, n_hg)),
            pltpu.SemaphoreType.DMA((WINDOW, n_hg)),
        ],
        compiler_params=pltpu.CompilerParams(
            collective_id=0, has_side_effects=True, vmem_limit_bytes=60 * 1024 * 1024
        ),
    )(block_mask, q.reshape(rows, latent), qr.transpose(1, 2, 0), kn, kr.T, g.reshape(rows, latent))
    return dq.reshape(tokens, heads, latent), dqr.transpose(2, 0, 1), dkn, dkr


def solution(mesh):
    wide = P("ctx", "hg", None)
    owned = P(("ctx", "hg"), None)
    return jax.shard_map(
        functools.partial(on_device, mesh.shape["ctx"], mesh.shape["hg"]),
        mesh=mesh,
        in_specs=(wide, wide, P("ctx", None), P("ctx", None), wide, P()),
        out_specs=(wide, wide, owned, owned),
        check_vma=False,
    )
```

```python
import functools
import math

import jax
import jax.numpy as jnp
from jax import lax
from jax.experimental import pallas as pl
from jax.experimental.pallas import tpu as pltpu
from jax.sharding import PartitionSpec as P

WINDOW = 4
PAIRS = WINDOW // 2
ORDER = (0, 2, 1, 3)
SCORE_SCALE = 192.0 ** (-0.5)
LOG2E = math.log2(math.e)
LANES = 128
MESH = pl.DeviceIdType.MESH


def dot_nn(a, b):
    return jnp.dot(a, b, preferred_element_type=jnp.float32)


def dot_nt(a, b):
    return lax.dot_general(a, b, (((1,), (1,)), ((), ())), preferred_element_type=jnp.float32)


def dot_tn(a, b):
    return lax.dot_general(a, b, (((0,), (0,)), ((), ())), preferred_element_type=jnp.float32)


def kernel(
    n_ctx,
    n_hg,
    mask_ref,
    q_hbm,
    qr_hbm,
    kn_hbm,
    kr_hbm,
    g_hbm,
    dq_ref,
    dqr_ref,
    dkn_ref,
    dkr_ref,
    q_ref,
    qrt_ref,
    qr_wide,
    qr_ref,
    g_ref,
    kn_all,
    krt_all,
    dq_tile,
    dqr_wide,
    dqrt_ref,
    x_ref,
    dp_ref,
    prob_ref,
    ds_ref,
    bias_ref,
    acc_ref,
    comb_out,
    comb_in,
    dk_out,
    dk_in,
    load_sem,
    store_sem,
    k_send,
    k_recv,
    c_sem,
    d_send,
    d_recv,
):
    rows, latent = q_ref.shape
    rope = qr_ref.shape[1]
    heads = qrt_ref.shape[0]
    tokens = qrt_ref.shape[2]
    keys = kn_all.shape[1]
    piece = keys // n_hg
    pair = 2 * keys
    blocks = mask_ref.shape[0] // n_ctx
    block_rows = rows // blocks
    tile = 512
    tiles = rows // tile
    soft_rows = 256
    sub_rows = 32
    c = lax.axis_index("ctx")
    h = lax.axis_index("hg")

    load_kn = pltpu.make_async_copy(kn_hbm, kn_all.at[0], load_sem.at[0])
    load_kr = pltpu.make_async_copy(kr_hbm, krt_all.at[0], load_sem.at[1])
    load_q = pltpu.make_async_copy(q_hbm, q_ref, load_sem.at[2])
    load_qr = pltpu.make_async_copy(qr_hbm, qrt_ref, load_sem.at[3])
    load_g = pltpu.make_async_copy(g_hbm, g_ref, load_sem.at[4])
    load_kn.start()
    load_kr.start()

    core = lax.rem(c, 2)
    sibling = c + 1 - 2 * core
    ahead = lax.rem(c + 2, n_ctx)
    behind = lax.rem(c + n_ctx - 2, n_ctx)
    far = lax.rem(c + n_ctx - 3 + 6 * core, n_ctx)

    barrier = pltpu.get_barrier_semaphore()
    greeted = 0
    for where in (c, sibling, ahead, behind, far):
        for k in range(n_hg):
            if where is c and k == 0:
                continue
            pl.semaphore_signal(
                barrier,
                inc=1,
                device_id=(where, lax.rem(h + k, n_hg)),
                device_id_type=MESH,
            )
            greeted += 1
    load_q.start()
    load_qr.start()
    load_g.start()

    load_kn.wait()
    load_kr.wait()
    pl.semaphore_wait(barrier, greeted)

    def latent_copy(source, place, target, kind):
        return [
            pltpu.make_async_remote_copy(
                src_ref=buffer.at[source],
                dst_ref=buffer.at[place],
                send_sem=k_send.at[kind, part],
                recv_sem=k_recv.at[place, part],
                device_id=(target, h),
                device_id_type=MESH,
            )
            for part, buffer in enumerate((kn_all, krt_all))
        ]

    to_ahead = latent_copy(0, 1, ahead, 0)
    to_other = latent_copy(0, 2 + core, lax.rem(c + 1 + 2 * core, n_ctx), 1)
    handed_on = latent_copy(1, 3 - core, sibling, 2)
    for copy in to_ahead + to_other:
        copy.start()

    def wait_latents(place):
        for copy in latent_copy(0, place, sibling, 0):
            copy.wait_recv()

    key_block = lax.broadcasted_iota(jnp.int32, (1, WINDOW * keys), 1) // (keys // blocks)
    for rb in range(blocks):
        bias = jnp.zeros((1, WINDOW * keys), jnp.float32)
        for place, d in enumerate(ORDER):
            source = lax.rem(c - d + n_ctx, n_ctx)
            for kb in range(blocks):
                bit = mask_ref[c * blocks + rb, source * blocks + kb]
                value = jnp.where(bit == 1, 0.0, -jnp.inf).astype(jnp.float32)
                bias = jnp.where(key_block == place * blocks + kb, value, bias)
        bias_ref[rb : rb + 1, :] = bias

    acc_ref[...] = jnp.zeros_like(acc_ref)
    load_qr.wait()
    for head in range(heads):
        turned = qrt_ref[head].astype(jnp.float32).T
        qr_wide[pl.ds(head, tokens, stride=heads), :] = turned
    qr_ref[...] = qr_wide[...].astype(qr_ref.dtype)
    load_q.wait()
    load_g.wait()

    for p in range(PAIRS):
        if p == 0:
            wait_latents(1)
            for copy in handed_on:
                copy.start()
        else:
            wait_latents(2)
            wait_latents(3)
        cols = slice(p * pair, (p + 1) * pair)

        def score_tile(i, _, p=p, cols=cols):
            r = pl.ds(pl.multiple_of(i * tile, tile), tile)
            kn = kn_all[2 * p : 2 * p + 2].reshape(pair, latent)
            krt = jnp.concatenate([krt_all[2 * p], krt_all[2 * p + 1]], axis=1)
            bias = bias_ref[pl.ds(i * tile // block_rows, 1), cols]
            s = dot_nt(q_ref[r, :], kn) + dot_nn(qr_ref[r, :], krt)
            x_ref[r, cols] = s * (SCORE_SCALE * LOG2E) + bias
            dp_ref[r, cols] = dot_nt(g_ref[r, :], kn)
            return 0

        lax.fori_loop(0, tiles, score_tile, 0)

    def add_key_grads(p, r, ds, prob):
        q = q_ref[r, :]
        acc_ref[p, :, :latent] += dot_tn(ds, q) + dot_tn(prob, g_ref[r, :])
        acc_ref[p, :, latent : latent + rope] += dot_tn(ds, qr_ref[r, :])

    def send_pieces(kind, target):
        out = []
        for k in reversed(range(n_hg)):
            if kind == 0 and k == 0:
                continue
            peer = lax.rem(h + k, n_hg)
            copy = pltpu.make_async_remote_copy(
                src_ref=dk_out.at[kind, peer],
                dst_ref=dk_in.at[kind, k],
                send_sem=d_send.at[kind, k],
                recv_sem=d_recv.at[kind, k],
                device_id=(target, peer),
                device_id_type=MESH,
            )
            copy.start()
            out.append((kind, k, copy))
        return out

    def split(block):
        return block.reshape(n_hg, piece, block.shape[1]).astype(dk_out.dtype)

    def half_of_last(which):
        return acc_ref[last, pl.ds(pl.multiple_of(which * keys, keys), keys), :]

    last = PAIRS - 1

    for start in range(0, rows, soft_rows):
        for at in range(start, start + soft_rows, sub_rows):
            r = slice(at, at + sub_rows)
            x = x_ref[r, :]
            dp = dp_ref[r, :]
            e = jnp.exp2(x - jnp.max(x, axis=1, keepdims=True))
            inv = 1.0 / jnp.sum(e, axis=1, keepdims=True)
            delta = jnp.sum(e * dp, axis=1, keepdims=True) * inv
            prob_ref[r, :] = (e * inv).astype(jnp.bfloat16)
            ds_ref[r, :] = (e * (inv * SCORE_SCALE) * (dp - delta)).astype(jnp.bfloat16)
        r = slice(start, start + soft_rows)
        cols = slice(last * pair, (last + 1) * pair)
        add_key_grads(last, r, ds_ref[r, cols], prob_ref[r, cols])
    comb_out[...] = half_of_last(core).astype(comb_out.dtype)
    combine = pltpu.make_async_remote_copy(
        src_ref=comb_out,
        dst_ref=comb_in,
        send_sem=c_sem.at[0],
        recv_sem=c_sem.at[1],
        device_id=(sibling, h),
        device_id_type=MESH,
    )
    combine.start()
    dk_out[2] = split(half_of_last(1 - core))
    moving = send_pieces(2, lax.rem(c + n_ctx - 3 + 2 * core, n_ctx))

    for p in reversed(range(last)):
        cols = slice(p * pair, (p + 1) * pair)

        def grad_tile(i, _, p=p, cols=cols):
            r = pl.ds(pl.multiple_of(i * tile, tile), tile)
            add_key_grads(p, r, ds_ref[r, cols], prob_ref[r, cols])
            return 0

        lax.fori_loop(0, tiles, grad_tile, 0)

    combine.wait_recv()
    dk_out[1] = split(acc_ref[0, keys:, :] + comb_in[...].astype(jnp.float32))
    moving += send_pieces(1, behind)
    dk_out[0] = split(acc_ref[0, :keys, :])
    moving += send_pieces(0, c)

    stores = []
    for i in range(tiles):
        r = slice(i * tile, (i + 1) * tile)
        ds = ds_ref[r, :]
        kn = kn_all[...].reshape(WINDOW * keys, latent)
        krt = jnp.concatenate([krt_all[d] for d in range(WINDOW)], axis=1)
        dq_tile[r, :] = dot_nn(ds, kn).astype(dq_tile.dtype)
        dqr_wide[r, :] = dot_nt(ds, krt)
        copy = pltpu.make_async_copy(dq_tile.at[r, :], dq_ref.at[r, :], store_sem.at[i])
        copy.start()
        stores.append(copy)
    for head in range(heads):
        part = dqr_wide[pl.ds(head, tokens, stride=heads), :]
        dqrt_ref[head] = part.T.astype(dqrt_ref.dtype)
    copy = pltpu.make_async_copy(dqrt_ref, dqr_ref, store_sem.at[tiles])
    copy.start()
    stores.append(copy)

    total = acc_ref[0, pl.ds(pl.multiple_of(h * piece, piece), piece), :]
    for kind, k, copy in sorted(moving, key=lambda m: (-m[0], m[1])):
        copy.wait_recv()
        total = total + dk_in[kind, k].astype(jnp.float32)
    dkn_ref[...] = total[:, :latent]
    dkr_ref[...] = total[:, latent : latent + rope]

    for copy in to_ahead + to_other + handed_on + [combine]:
        copy.wait_send()
    for copy in stores:
        copy.wait()
    for _, _, copy in moving:
        copy.wait_send()


def hand_over(dq_in, dqr_in, dkn_in, dkr_in, dq_ref, dqr_ref, dkn_ref, dkr_ref, dq, dqr, dkn, dkr, load_sem, store_sem):
    parts = []
    rows = dq.shape[0]
    step = rows // 4
    for at in range(0, rows, step):
        r = pl.ds(at, step)
        parts.append((dq_in.at[r, :], dq.at[r, :], dq_ref.at[r, :]))
    parts += [(dqr_in, dqr, dqr_ref), (dkn_in, dkn, dkn_ref), (dkr_in, dkr, dkr_ref)]
    loads = [pltpu.make_async_copy(a, b, load_sem.at[i]) for i, (a, b, _) in enumerate(parts)]
    stores = [pltpu.make_async_copy(b, o, store_sem.at[i]) for i, (_, b, o) in enumerate(parts)]
    for load in loads:
        load.start()
    for load, store in zip(loads, stores):
        load.wait()
        store.start()
    for store in stores:
        store.wait()


def on_device(n_ctx, n_hg, q, qr, kn, kr, g, block_mask):
    tokens, heads, latent = q.shape
    rope = qr.shape[2]
    rows = tokens * heads
    width = -(-(latent + rope) // LANES) * LANES
    piece = tokens // n_hg
    blocks = block_mask.shape[0] // n_ctx
    bf16, f32 = jnp.bfloat16, jnp.float32
    hbm = pl.BlockSpec(memory_space=pl.ANY)
    vmem = pl.BlockSpec(memory_space=pltpu.VMEM)
    dq, dqr, dkn, dkr = pl.pallas_call(
        functools.partial(kernel, n_ctx, n_hg),
        out_shape=(
            jax.ShapeDtypeStruct((rows, latent), bf16),
            jax.ShapeDtypeStruct((heads, rope, tokens), bf16),
            jax.ShapeDtypeStruct((piece, latent), f32),
            jax.ShapeDtypeStruct((piece, rope), f32),
        ),
        in_specs=[pl.BlockSpec(memory_space=pltpu.SMEM)] + [hbm] * 5,
        out_specs=[hbm, hbm, vmem, vmem],
        scratch_shapes=[
            pltpu.VMEM((rows, latent), bf16),
            pltpu.VMEM((heads, rope, tokens), bf16),
            pltpu.VMEM((rows, rope), f32),
            pltpu.VMEM((rows, rope), bf16),
            pltpu.VMEM((rows, latent), bf16),
            pltpu.VMEM((WINDOW, tokens, latent), bf16),
            pltpu.VMEM((WINDOW, rope, tokens), bf16),
            pltpu.VMEM((rows, latent), bf16),
            pltpu.VMEM((rows, rope), f32),
            pltpu.VMEM((heads, rope, tokens), bf16),
            pltpu.VMEM((rows, WINDOW * tokens), f32),
            pltpu.VMEM((rows, WINDOW * tokens), f32),
            pltpu.VMEM((rows, WINDOW * tokens), bf16),
            pltpu.VMEM((rows, WINDOW * tokens), bf16),
            pltpu.VMEM((blocks, WINDOW * tokens), f32),
            pltpu.VMEM((PAIRS, 2 * tokens, width), f32),
            pltpu.VMEM((tokens, width), bf16),
            pltpu.VMEM((tokens, width), bf16),
            pltpu.VMEM((3, n_hg, piece, width), bf16),
            pltpu.VMEM((3, n_hg, piece, width), bf16),
            pltpu.SemaphoreType.DMA((5,)),
            pltpu.SemaphoreType.DMA((rows // 512 + 1,)),
            pltpu.SemaphoreType.DMA((WINDOW, 2)),
            pltpu.SemaphoreType.DMA((WINDOW, 2)),
            pltpu.SemaphoreType.DMA((2,)),
            pltpu.SemaphoreType.DMA((3, n_hg)),
            pltpu.SemaphoreType.DMA((3, n_hg)),
        ],
        compiler_params=pltpu.CompilerParams(
            collective_id=0, has_side_effects=True, vmem_limit_bytes=60 * 1024 * 1024
        ),
    )(block_mask, q.reshape(rows, latent), qr.transpose(1, 2, 0), kn, kr.T, g.reshape(rows, latent))
    made = (dq, dqr, dkn, dkr)
    dq, dqr, dkn, dkr = pl.pallas_call(
        hand_over,
        out_shape=tuple(jax.ShapeDtypeStruct(a.shape, a.dtype) for a in made),
        in_specs=[hbm] * 4,
        out_specs=[hbm] * 4,
        scratch_shapes=[pltpu.VMEM(a.shape, a.dtype) for a in made]
        + [pltpu.SemaphoreType.DMA((7,)), pltpu.SemaphoreType.DMA((7,))],
        compiler_params=pltpu.CompilerParams(vmem_limit_bytes=60 * 1024 * 1024),
    )(*made)
    return dq.reshape(tokens, heads, latent), dqr.transpose(2, 0, 1), dkn, dkr


def solution(mesh):
    wide = P("ctx", "hg", None)
    owned = P(("ctx", "hg"), None)
    return jax.shard_map(
        functools.partial(on_device, mesh.shape["ctx"], mesh.shape["hg"]),
        mesh=mesh,
        in_specs=(wide, wide, P("ctx", None), P("ctx", None), wide, P()),
        out_specs=(wide, wide, owned, owned),
        check_vma=False,
    )
```

```python
import functools
import math

import jax
import jax.numpy as jnp
from jax import lax
from jax.experimental import pallas as pl
from jax.experimental.pallas import tpu as pltpu
from jax.sharding import PartitionSpec as P

WINDOW = 4
PAIRS = WINDOW // 2
ORDER = (0, 2, 1, 3)
SCORE_SCALE = 192.0 ** (-0.5)
LOG2E = math.log2(math.e)
LANES = 128
MESH = pl.DeviceIdType.MESH


def dot_nn(a, b):
    return jnp.dot(a, b, preferred_element_type=jnp.float32)


def dot_nt(a, b):
    return lax.dot_general(a, b, (((1,), (1,)), ((), ())), preferred_element_type=jnp.float32)


def dot_tn(a, b):
    return lax.dot_general(a, b, (((0,), (0,)), ((), ())), preferred_element_type=jnp.float32)


def kernel(
    n_ctx,
    n_hg,
    mask_ref,
    q_hbm,
    qr_hbm,
    kn_hbm,
    kr_hbm,
    g_hbm,
    dq_ref,
    dqr_ref,
    dkn_ref,
    dkr_ref,
    q_ref,
    qrt_ref,
    qr_wide,
    qr_ref,
    g_ref,
    kn_all,
    krt_all,
    kr_all,
    dq_tile,
    dqr_wide,
    dqrt_ref,
    x_ref,
    dp_ref,
    prob_ref,
    ds_ref,
    top_ref,
    acc_ref,
    comb_out,
    comb_in,
    dk_out,
    dk_in,
    load_sem,
    store_sem,
    k_send,
    k_recv,
    c_sem,
    d_send,
    d_recv,
):
    rows, latent = q_ref.shape
    rope = qr_ref.shape[1]
    heads = qrt_ref.shape[0]
    tokens = qrt_ref.shape[2]
    keys = kn_all.shape[1]
    piece = keys // n_hg
    pair = 2 * keys
    blocks = mask_ref.shape[0] // n_ctx
    block_rows = rows // blocks
    tile = 512
    tiles = rows // tile
    group = 256
    chunk = keys // blocks
    c = lax.axis_index("ctx")
    h = lax.axis_index("hg")

    load_kn = pltpu.make_async_copy(kn_hbm, kn_all.at[0], load_sem.at[0])
    load_kr = pltpu.make_async_copy(kr_hbm, krt_all.at[0], load_sem.at[1])
    load_q = pltpu.make_async_copy(q_hbm, q_ref, load_sem.at[2])
    load_qr = pltpu.make_async_copy(qr_hbm, qrt_ref, load_sem.at[3])
    load_g = pltpu.make_async_copy(g_hbm, g_ref, load_sem.at[4])
    load_kn.start()
    load_kr.start()

    core = lax.rem(c, 2)
    sibling = c + 1 - 2 * core
    ahead = lax.rem(c + 2, n_ctx)
    behind = lax.rem(c + n_ctx - 2, n_ctx)
    far = lax.rem(c + n_ctx - 3 + 6 * core, n_ctx)

    barrier = pltpu.get_barrier_semaphore()
    greeted = 0
    for where in (c, sibling, ahead, behind, far):
        for k in range(n_hg):
            if where is c and k == 0:
                continue
            pl.semaphore_signal(
                barrier,
                inc=1,
                device_id=(where, lax.rem(h + k, n_hg)),
                device_id_type=MESH,
            )
            greeted += 1
    load_q.start()
    load_qr.start()
    load_g.start()

    load_kn.wait()
    load_kr.wait()
    pl.semaphore_wait(barrier, greeted)

    def latent_copy(source, place, target, kind):
        return [
            pltpu.make_async_remote_copy(
                src_ref=buffer.at[source],
                dst_ref=buffer.at[place],
                send_sem=k_send.at[kind, part],
                recv_sem=k_recv.at[place, part],
                device_id=(target, h),
                device_id_type=MESH,
            )
            for part, buffer in enumerate((kn_all, krt_all))
        ]

    to_ahead = latent_copy(0, 1, ahead, 0)
    to_other = latent_copy(0, 2 + core, lax.rem(c + 1 + 2 * core, n_ctx), 1)
    handed_on = latent_copy(1, 3 - core, sibling, 2)
    for copy in to_ahead + to_other:
        copy.start()

    def wait_latents(place):
        for copy in latent_copy(0, place, sibling, 0):
            copy.wait_recv()

    bias = []
    for rb in range(blocks):
        for place, d in enumerate(ORDER):
            source = lax.rem(c - d + n_ctx, n_ctx)
            for kb in range(blocks):
                bit = mask_ref[c * blocks + rb, source * blocks + kb]
                bias.append(jnp.where(bit == 1, 0.0, -jnp.inf).astype(jnp.float32))

    acc_ref[...] = jnp.zeros_like(acc_ref)
    load_qr.wait()
    for head in range(heads):
        turned = qrt_ref[head].astype(jnp.float32).T
        qr_wide[pl.ds(head, tokens, stride=heads), :] = turned
    qr_ref[...] = qr_wide[...].astype(qr_ref.dtype)
    load_q.wait()
    load_g.wait()

    def turn_rope(place):
        kr_all[place] = krt_all[place].astype(jnp.float32).T.astype(kr_all.dtype)

    turn_rope(0)
    for p in range(PAIRS):
        if p == 0:
            wait_latents(1)
            for copy in handed_on:
                copy.start()
            turn_rope(1)
        else:
            for place in (2, 3):
                wait_latents(place)
                turn_rope(place)
        kn = kn_all[2 * p : 2 * p + 2].reshape(pair, latent)
        kr = kr_all[2 * p : 2 * p + 2].reshape(pair, rope)
        for i in range(tiles):
            r = slice(i * tile, (i + 1) * tile)
            rb = i * tile // block_rows
            s = dot_nt(kn, q_ref[r, :]) + dot_nt(kr, qr_ref[r, :])
            top = None
            for j in range(pair // chunk):
                number = (rb * WINDOW + 2 * p) * blocks + j
                x = s[j * chunk : (j + 1) * chunk, :] * (SCORE_SCALE * LOG2E) + bias[number]
                x_ref[p * pair + j * chunk : p * pair + (j + 1) * chunk, r] = x
                part = jnp.max(x.reshape(chunk // 8, 8, tile), axis=0)
                top = part if top is None else jnp.maximum(top, part)
            top_ref[8 * p : 8 * p + 8, r] = top
            dp_ref[p * pair : (p + 1) * pair, r] = dot_nt(kn, g_ref[r, :])

    def add_key_grads(p, r):
        ds = ds_ref[p * pair : (p + 1) * pair, r]
        prob = prob_ref[p * pair : (p + 1) * pair, r]
        acc_ref[p, :, :latent] += dot_nn(ds, q_ref[r, :]) + dot_nn(prob, g_ref[r, :])
        acc_ref[p, :, latent : latent + rope] += dot_nn(ds, qr_ref[r, :])

    def send_pieces(kind, target):
        out = []
        for k in reversed(range(n_hg)):
            if kind == 0 and k == 0:
                continue
            peer = lax.rem(h + k, n_hg)
            copy = pltpu.make_async_remote_copy(
                src_ref=dk_out.at[kind, peer],
                dst_ref=dk_in.at[kind, k],
                send_sem=d_send.at[kind, k],
                recv_sem=d_recv.at[kind, k],
                device_id=(target, peer),
                device_id_type=MESH,
            )
            copy.start()
            out.append((kind, k, copy))
        return out

    def split(block):
        return block.reshape(n_hg, piece, block.shape[1]).astype(dk_out.dtype)

    def half_of_last(which):
        return acc_ref[last, pl.ds(pl.multiple_of(which * keys, keys), keys), :]

    last = PAIRS - 1

    def folded(a):
        return jnp.sum(a.reshape(a.shape[0] // 8, 8, a.shape[1]), axis=0)

    for start in range(0, rows, tile):
        for at in range(start, start + tile, group):
            r = slice(at, at + group)
            top = jnp.max(top_ref[:, r], axis=0, keepdims=True)
            total = jnp.zeros((8, group), jnp.float32)
            mixed = jnp.zeros((8, group), jnp.float32)
            for k in range(0, WINDOW * keys, chunk):
                e = jnp.exp2(x_ref[k : k + chunk, r] - top)
                x_ref[k : k + chunk, r] = e
                total += folded(e)
                mixed += folded(e * dp_ref[k : k + chunk, r])
            inv = 1.0 / jnp.sum(total, axis=0, keepdims=True)
            delta = jnp.sum(mixed, axis=0, keepdims=True) * inv
            scaled = inv * SCORE_SCALE
            for k in range(0, WINDOW * keys, chunk):
                e = x_ref[k : k + chunk, r]
                prob_ref[k : k + chunk, r] = (e * inv).astype(jnp.bfloat16)
                ds = (e * scaled) * (dp_ref[k : k + chunk, r] - delta)
                ds_ref[k : k + chunk, r] = ds.astype(jnp.bfloat16)
        add_key_grads(last, slice(start, start + tile))
    comb_out[...] = half_of_last(core).astype(comb_out.dtype)
    combine = pltpu.make_async_remote_copy(
        src_ref=comb_out,
        dst_ref=comb_in,
        send_sem=c_sem.at[0],
        recv_sem=c_sem.at[1],
        device_id=(sibling, h),
        device_id_type=MESH,
    )
    combine.start()
    dk_out[2] = split(half_of_last(1 - core))
    moving = send_pieces(2, lax.rem(c + n_ctx - 3 + 2 * core, n_ctx))

    for p in reversed(range(last)):
        for start in range(0, rows, 2 * tile):
            add_key_grads(p, slice(start, start + 2 * tile))

    combine.wait_recv()
    dk_out[1] = split(acc_ref[0, keys:, :] + comb_in[...].astype(jnp.float32))
    moving += send_pieces(1, behind)
    dk_out[0] = split(acc_ref[0, :keys, :])
    moving += send_pieces(0, c)

    stores = []
    for i in range(tiles):
        r = slice(i * tile, (i + 1) * tile)
        ds = ds_ref[:, r]
        dq_tile[r, :] = dot_tn(ds, kn_all[...].reshape(WINDOW * keys, latent)).astype(dq_tile.dtype)
        dqr_wide[r, :] = dot_tn(ds, kr_all[...].reshape(WINDOW * keys, rope))
        copy = pltpu.make_async_copy(dq_tile.at[r, :], dq_ref.at[r, :], store_sem.at[i])
        copy.start()
        stores.append(copy)
    for head in range(heads):
        part = dqr_wide[pl.ds(head, tokens, stride=heads), :]
        dqrt_ref[head] = part.T.astype(dqrt_ref.dtype)
    copy = pltpu.make_async_copy(dqrt_ref, dqr_ref, store_sem.at[tiles])
    copy.start()
    stores.append(copy)

    total = acc_ref[0, pl.ds(pl.multiple_of(h * piece, piece), piece), :]
    for kind, k, copy in sorted(moving, key=lambda m: (-m[0], m[1])):
        copy.wait_recv()
        total = total + dk_in[kind, k].astype(jnp.float32)
    dkn_ref[...] = total[:, :latent]
    dkr_ref[...] = total[:, latent : latent + rope]

    for copy in to_ahead + to_other + handed_on + [combine]:
        copy.wait_send()
    for copy in stores:
        copy.wait()
    for _, _, copy in moving:
        copy.wait_send()


def hand_over(dq_in, dqr_in, dkn_in, dkr_in, dq_ref, dqr_ref, dkn_ref, dkr_ref, dq, dqr, dkn, dkr, load_sem, store_sem):
    parts = []
    rows = dq.shape[0]
    step = rows // 4
    for at in range(0, rows, step):
        r = pl.ds(at, step)
        parts.append((dq_in.at[r, :], dq.at[r, :], dq_ref.at[r, :]))
    parts += [(dqr_in, dqr, dqr_ref), (dkn_in, dkn, dkn_ref), (dkr_in, dkr, dkr_ref)]
    loads = [pltpu.make_async_copy(a, b, load_sem.at[i]) for i, (a, b, _) in enumerate(parts)]
    stores = [pltpu.make_async_copy(b, o, store_sem.at[i]) for i, (_, b, o) in enumerate(parts)]
    for load in loads:
        load.start()
    for load, store in zip(loads, stores):
        load.wait()
        store.start()
    for store in stores:
        store.wait()


def on_device(n_ctx, n_hg, q, qr, kn, kr, g, block_mask):
    tokens, heads, latent = q.shape
    rope = qr.shape[2]
    rows = tokens * heads
    width = -(-(latent + rope) // LANES) * LANES
    piece = tokens // n_hg
    blocks = block_mask.shape[0] // n_ctx
    bf16, f32 = jnp.bfloat16, jnp.float32
    hbm = pl.BlockSpec(memory_space=pl.ANY)
    vmem = pl.BlockSpec(memory_space=pltpu.VMEM)
    dq, dqr, dkn, dkr = pl.pallas_call(
        functools.partial(kernel, n_ctx, n_hg),
        out_shape=(
            jax.ShapeDtypeStruct((rows, latent), bf16),
            jax.ShapeDtypeStruct((heads, rope, tokens), bf16),
            jax.ShapeDtypeStruct((piece, latent), f32),
            jax.ShapeDtypeStruct((piece, rope), f32),
        ),
        in_specs=[pl.BlockSpec(memory_space=pltpu.SMEM)] + [hbm] * 5,
        out_specs=[hbm, hbm, vmem, vmem],
        scratch_shapes=[
            pltpu.VMEM((rows, latent), bf16),
            pltpu.VMEM((heads, rope, tokens), bf16),
            pltpu.VMEM((rows, rope), f32),
            pltpu.VMEM((rows, rope), bf16),
            pltpu.VMEM((rows, latent), bf16),
            pltpu.VMEM((WINDOW, tokens, latent), bf16),
            pltpu.VMEM((WINDOW, rope, tokens), bf16),
            pltpu.VMEM((WINDOW, tokens, rope), bf16),
            pltpu.VMEM((rows, latent), bf16),
            pltpu.VMEM((rows, rope), f32),
            pltpu.VMEM((heads, rope, tokens), bf16),
            pltpu.VMEM((WINDOW * tokens, rows), f32),
            pltpu.VMEM((WINDOW * tokens, rows), f32),
            pltpu.VMEM((WINDOW * tokens, rows), bf16),
            pltpu.VMEM((WINDOW * tokens, rows), bf16),
            pltpu.VMEM((8 * PAIRS, rows), f32),
            pltpu.VMEM((PAIRS, 2 * tokens, width), f32),
            pltpu.VMEM((tokens, width), bf16),
            pltpu.VMEM((tokens, width), bf16),
            pltpu.VMEM((3, n_hg, piece, width), bf16),
            pltpu.VMEM((3, n_hg, piece, width), bf16),
            pltpu.SemaphoreType.DMA((5,)),
            pltpu.SemaphoreType.DMA((rows // 512 + 1,)),
            pltpu.SemaphoreType.DMA((WINDOW, 2)),
            pltpu.SemaphoreType.DMA((WINDOW, 2)),
            pltpu.SemaphoreType.DMA((2,)),
            pltpu.SemaphoreType.DMA((3, n_hg)),
            pltpu.SemaphoreType.DMA((3, n_hg)),
        ],
        compiler_params=pltpu.CompilerParams(
            collective_id=0, has_side_effects=True, vmem_limit_bytes=60 * 1024 * 1024
        ),
    )(block_mask, q.reshape(rows, latent), qr.transpose(1, 2, 0), kn, kr.T, g.reshape(rows, latent))
    made = (dq, dqr, dkn, dkr)
    dq, dqr, dkn, dkr = pl.pallas_call(
        hand_over,
        out_shape=tuple(jax.ShapeDtypeStruct(a.shape, a.dtype) for a in made),
        in_specs=[hbm] * 4,
        out_specs=[hbm] * 4,
        scratch_shapes=[pltpu.VMEM(a.shape, a.dtype) for a in made]
        + [pltpu.SemaphoreType.DMA((7,)), pltpu.SemaphoreType.DMA((7,))],
        compiler_params=pltpu.CompilerParams(vmem_limit_bytes=60 * 1024 * 1024),
    )(*made)
    return dq.reshape(tokens, heads, latent), dqr.transpose(2, 0, 1), dkn, dkr


def solution(mesh):
    wide = P("ctx", "hg", None)
    owned = P(("ctx", "hg"), None)
    return jax.shard_map(
        functools.partial(on_device, mesh.shape["ctx"], mesh.shape["hg"]),
        mesh=mesh,
        in_specs=(wide, wide, P("ctx", None), P("ctx", None), wide, P()),
        out_specs=(wide, wide, owned, owned),
        check_vma=False,
    )
```

```python
import functools
import math

import jax
import jax.numpy as jnp
from jax import lax
from jax.experimental import pallas as pl
from jax.experimental.pallas import tpu as pltpu
from jax.sharding import PartitionSpec as P

WINDOW = 4
PAIRS = WINDOW // 2
ORDER = (0, 2, 1, 3)
SCORE_SCALE = 192.0 ** (-0.5)
LOG2E = math.log2(math.e)
LANES = 128
MESH = pl.DeviceIdType.MESH


def dot_nn(a, b):
    return jnp.dot(a, b, preferred_element_type=jnp.float32)


def dot_nt(a, b):
    return lax.dot_general(a, b, (((1,), (1,)), ((), ())), preferred_element_type=jnp.float32)


def dot_tn(a, b):
    return lax.dot_general(a, b, (((0,), (0,)), ((), ())), preferred_element_type=jnp.float32)


def kernel(
    n_ctx,
    n_hg,
    mask_ref,
    q_hbm,
    qr_hbm,
    kn_hbm,
    kr_hbm,
    g_hbm,
    dq_ref,
    dqr_ref,
    dkn_ref,
    dkr_ref,
    q_ref,
    qrt_ref,
    qr_wide,
    qr_ref,
    g_ref,
    kn_all,
    krt_all,
    kr_all,
    dq_tile,
    dqr_wide,
    dqrt_ref,
    x_ref,
    dp_ref,
    prob_ref,
    ds_ref,
    top_ref,
    acc_ref,
    comb_out,
    comb_in,
    dk_out,
    dk_in,
    load_sem,
    store_sem,
    k_send,
    k_recv,
    c_sem,
    d_send,
    d_recv,
):
    rows, latent = q_ref.shape
    rope = qr_ref.shape[1]
    heads = qrt_ref.shape[0]
    tokens = qrt_ref.shape[2]
    keys = kn_all.shape[1]
    piece = keys // n_hg
    pair = 2 * keys
    blocks = mask_ref.shape[0] // n_ctx
    block_rows = rows // blocks
    tile = 512
    tiles = rows // tile
    group = 256
    chunk = keys // blocks
    c = lax.axis_index("ctx")
    h = lax.axis_index("hg")

    load_kn = pltpu.make_async_copy(kn_hbm, kn_all.at[0], load_sem.at[0])
    load_kr = pltpu.make_async_copy(kr_hbm, krt_all.at[0], load_sem.at[1])
    load_q = pltpu.make_async_copy(q_hbm, q_ref, load_sem.at[2])
    load_qr = pltpu.make_async_copy(qr_hbm, qrt_ref, load_sem.at[3])
    load_g = pltpu.make_async_copy(g_hbm, g_ref, load_sem.at[4])
    load_kn.start()
    load_kr.start()

    core = lax.rem(c, 2)
    sibling = c + 1 - 2 * core
    ahead = lax.rem(c + 2, n_ctx)
    behind = lax.rem(c + n_ctx - 2, n_ctx)
    far = lax.rem(c + n_ctx - 3 + 6 * core, n_ctx)

    barrier = pltpu.get_barrier_semaphore()
    greeted = 0
    for where in (c, sibling, ahead, behind, far):
        for k in range(n_hg):
            if where is c and k == 0:
                continue
            pl.semaphore_signal(
                barrier,
                inc=1,
                device_id=(where, lax.rem(h + k, n_hg)),
                device_id_type=MESH,
            )
            greeted += 1
    load_q.start()
    load_qr.start()
    load_g.start()

    load_kn.wait()
    load_kr.wait()
    pl.semaphore_wait(barrier, greeted)

    def latent_copy(source, place, target, kind):
        return [
            pltpu.make_async_remote_copy(
                src_ref=buffer.at[source],
                dst_ref=buffer.at[place],
                send_sem=k_send.at[kind, part],
                recv_sem=k_recv.at[place, part],
                device_id=(target, h),
                device_id_type=MESH,
            )
            for part, buffer in enumerate((kn_all, krt_all))
        ]

    to_ahead = latent_copy(0, 1, ahead, 0)
    to_other = latent_copy(0, 2 + core, lax.rem(c + 1 + 2 * core, n_ctx), 1)
    handed_on = latent_copy(1, 3 - core, sibling, 2)
    for copy in to_ahead + to_other:
        copy.start()

    def wait_latents(place):
        for copy in latent_copy(0, place, sibling, 0):
            copy.wait_recv()

    bias = []
    for rb in range(blocks):
        for place, d in enumerate(ORDER):
            source = lax.rem(c - d + n_ctx, n_ctx)
            for kb in range(blocks):
                bit = mask_ref[c * blocks + rb, source * blocks + kb]
                bias.append(jnp.where(bit == 1, 0.0, -jnp.inf).astype(jnp.float32))

    acc_ref[...] = jnp.zeros_like(acc_ref)
    load_qr.wait()
    for head in range(heads):
        turned = qrt_ref[head].astype(jnp.float32).T
        qr_wide[pl.ds(head, tokens, stride=heads), :] = turned
    qr_ref[...] = qr_wide[...].astype(qr_ref.dtype)
    load_q.wait()
    load_g.wait()

    def turn_rope(place):
        kr_all[place] = krt_all[place].astype(jnp.float32).T.astype(kr_all.dtype)

    turn_rope(0)
    for p in range(PAIRS):
        if p == 0:
            wait_latents(1)
            for copy in handed_on:
                copy.start()
            turn_rope(1)
        else:
            for place in (2, 3):
                wait_latents(place)
                turn_rope(place)
        kn = kn_all[2 * p : 2 * p + 2].reshape(pair, latent)
        kr = kr_all[2 * p : 2 * p + 2].reshape(pair, rope)
        for i in range(tiles):
            r = slice(i * tile, (i + 1) * tile)
            rb = i * tile // block_rows
            s = dot_nt(kn, q_ref[r, :]) + dot_nt(kr, qr_ref[r, :])
            top = None
            for j in range(pair // chunk):
                number = (rb * WINDOW + 2 * p) * blocks + j
                x = s[j * chunk : (j + 1) * chunk, :] * (SCORE_SCALE * LOG2E) + bias[number]
                x_ref[p * pair + j * chunk : p * pair + (j + 1) * chunk, r] = x
                part = jnp.max(x.reshape(chunk // 8, 8, tile), axis=0)
                top = part if top is None else jnp.maximum(top, part)
            top_ref[8 * p : 8 * p + 8, r] = top
            dp_ref[p * pair : (p + 1) * pair, r] = dot_nt(kn, g_ref[r, :])

    def add_key_grads(r):
        ds = ds_ref[:, r]
        acc_ref[:, :latent] += dot_nn(ds, q_ref[r, :]) + dot_nn(prob_ref[:, r], g_ref[r, :])
        acc_ref[:, latent : latent + rope] += dot_nn(ds, qr_ref[r, :])

    def send_pieces(kind, target):
        out = []
        for k in reversed(range(n_hg)):
            if kind == 0 and k == 0:
                continue
            peer = lax.rem(h + k, n_hg)
            copy = pltpu.make_async_remote_copy(
                src_ref=dk_out.at[kind, peer],
                dst_ref=dk_in.at[kind, k],
                send_sem=d_send.at[kind, k],
                recv_sem=d_recv.at[kind, k],
                device_id=(target, peer),
                device_id_type=MESH,
            )
            copy.start()
            out.append((kind, k, copy))
        return out

    def split(block):
        return block.reshape(n_hg, piece, block.shape[1]).astype(dk_out.dtype)

    def one_of_last(which):
        return acc_ref[pl.ds(pl.multiple_of(pair + which * keys, keys), keys), :]

    def folded(a):
        return jnp.sum(a.reshape(a.shape[0] // 8, 8, a.shape[1]), axis=0)

    for start in range(0, rows, tile):
        for at in range(start, start + tile, group):
            r = slice(at, at + group)
            top = jnp.max(top_ref[:, r], axis=0, keepdims=True)
            total = jnp.zeros((8, group), jnp.float32)
            mixed = jnp.zeros((8, group), jnp.float32)
            for k in range(0, WINDOW * keys, chunk):
                e = jnp.exp2(x_ref[k : k + chunk, r] - top)
                x_ref[k : k + chunk, r] = e
                total += folded(e)
                mixed += folded(e * dp_ref[k : k + chunk, r])
            inv = 1.0 / jnp.sum(total, axis=0, keepdims=True)
            delta = jnp.sum(mixed, axis=0, keepdims=True) * inv
            scaled = inv * SCORE_SCALE
            for k in range(0, WINDOW * keys, chunk):
                e = x_ref[k : k + chunk, r]
                prob_ref[k : k + chunk, r] = (e * inv).astype(jnp.bfloat16)
                ds = (e * scaled) * (dp_ref[k : k + chunk, r] - delta)
                ds_ref[k : k + chunk, r] = ds.astype(jnp.bfloat16)
        if start > 0:
            add_key_grads(slice(start - tile, start))
    add_key_grads(slice(rows - tile, rows))
    comb_out[...] = one_of_last(core).astype(comb_out.dtype)
    combine = pltpu.make_async_remote_copy(
        src_ref=comb_out,
        dst_ref=comb_in,
        send_sem=c_sem.at[0],
        recv_sem=c_sem.at[1],
        device_id=(sibling, h),
        device_id_type=MESH,
    )
    combine.start()
    dk_out[2] = split(one_of_last(1 - core))
    moving = send_pieces(2, lax.rem(c + n_ctx - 3 + 2 * core, n_ctx))

    dk_out[0] = split(acc_ref[:keys, :])
    moving += send_pieces(0, c)
    combine.wait_recv()
    dk_out[1] = split(acc_ref[keys:pair, :] + comb_in[...].astype(jnp.float32))
    moving += send_pieces(1, behind)

    stores = []
    for i in range(tiles):
        r = slice(i * tile, (i + 1) * tile)
        ds = ds_ref[:, r]
        dq_tile[r, :] = dot_tn(ds, kn_all[...].reshape(WINDOW * keys, latent)).astype(dq_tile.dtype)
        dqr_wide[r, :] = dot_tn(ds, kr_all[...].reshape(WINDOW * keys, rope))
        copy = pltpu.make_async_copy(dq_tile.at[r, :], dq_ref.at[r, :], store_sem.at[i])
        copy.start()
        stores.append(copy)
    for head in range(heads):
        part = dqr_wide[pl.ds(head, tokens, stride=heads), :]
        dqrt_ref[head] = part.T.astype(dqrt_ref.dtype)
    copy = pltpu.make_async_copy(dqrt_ref, dqr_ref, store_sem.at[tiles])
    copy.start()
    stores.append(copy)

    total = acc_ref[pl.ds(pl.multiple_of(h * piece, piece), piece), :]
    for kind, k, copy in sorted(moving, key=lambda m: (-m[0], m[1])):
        copy.wait_recv()
        total = total + dk_in[kind, k].astype(jnp.float32)
    dkn_ref[...] = total[:, :latent]
    dkr_ref[...] = total[:, latent : latent + rope]

    for copy in to_ahead + to_other + handed_on + [combine]:
        copy.wait_send()
    for copy in stores:
        copy.wait()
    for _, _, copy in moving:
        copy.wait_send()


def hand_over(dq_in, dqr_in, dkn_in, dkr_in, dq_ref, dqr_ref, dkn_ref, dkr_ref, dq, dqr, dkn, dkr, load_sem, store_sem):
    parts = []
    rows = dq.shape[0]
    step = rows // 4
    for at in range(0, rows, step):
        r = pl.ds(at, step)
        parts.append((dq_in.at[r, :], dq.at[r, :], dq_ref.at[r, :]))
    parts += [(dqr_in, dqr, dqr_ref), (dkn_in, dkn, dkn_ref), (dkr_in, dkr, dkr_ref)]
    loads = [pltpu.make_async_copy(a, b, load_sem.at[i]) for i, (a, b, _) in enumerate(parts)]
    stores = [pltpu.make_async_copy(b, o, store_sem.at[i]) for i, (_, b, o) in enumerate(parts)]
    for load in loads:
        load.start()
    for load, store in zip(loads, stores):
        load.wait()
        store.start()
    for store in stores:
        store.wait()


def on_device(n_ctx, n_hg, q, qr, kn, kr, g, block_mask):
    tokens, heads, latent = q.shape
    rope = qr.shape[2]
    rows = tokens * heads
    width = -(-(latent + rope) // LANES) * LANES
    piece = tokens // n_hg
    blocks = block_mask.shape[0] // n_ctx
    bf16, f32 = jnp.bfloat16, jnp.float32
    hbm = pl.BlockSpec(memory_space=pl.ANY)
    vmem = pl.BlockSpec(memory_space=pltpu.VMEM)
    dq, dqr, dkn, dkr = pl.pallas_call(
        functools.partial(kernel, n_ctx, n_hg),
        out_shape=(
            jax.ShapeDtypeStruct((rows, latent), bf16),
            jax.ShapeDtypeStruct((heads, rope, tokens), bf16),
            jax.ShapeDtypeStruct((piece, latent), f32),
            jax.ShapeDtypeStruct((piece, rope), f32),
        ),
        in_specs=[pl.BlockSpec(memory_space=pltpu.SMEM)] + [hbm] * 5,
        out_specs=[hbm, hbm, vmem, vmem],
        scratch_shapes=[
            pltpu.VMEM((rows, latent), bf16),
            pltpu.VMEM((heads, rope, tokens), bf16),
            pltpu.VMEM((rows, rope), f32),
            pltpu.VMEM((rows, rope), bf16),
            pltpu.VMEM((rows, latent), bf16),
            pltpu.VMEM((WINDOW, tokens, latent), bf16),
            pltpu.VMEM((WINDOW, rope, tokens), bf16),
            pltpu.VMEM((WINDOW, tokens, rope), bf16),
            pltpu.VMEM((rows, latent), bf16),
            pltpu.VMEM((rows, rope), f32),
            pltpu.VMEM((heads, rope, tokens), bf16),
            pltpu.VMEM((WINDOW * tokens, rows), f32),
            pltpu.VMEM((WINDOW * tokens, rows), f32),
            pltpu.VMEM((WINDOW * tokens, rows), bf16),
            pltpu.VMEM((WINDOW * tokens, rows), bf16),
            pltpu.VMEM((8 * PAIRS, rows), f32),
            pltpu.VMEM((WINDOW * tokens, width), f32),
            pltpu.VMEM((tokens, width), bf16),
            pltpu.VMEM((tokens, width), bf16),
            pltpu.VMEM((3, n_hg, piece, width), bf16),
            pltpu.VMEM((3, n_hg, piece, width), bf16),
            pltpu.SemaphoreType.DMA((5,)),
            pltpu.SemaphoreType.DMA((rows // 512 + 1,)),
            pltpu.SemaphoreType.DMA((WINDOW, 2)),
            pltpu.SemaphoreType.DMA((WINDOW, 2)),
            pltpu.SemaphoreType.DMA((2,)),
            pltpu.SemaphoreType.DMA((3, n_hg)),
            pltpu.SemaphoreType.DMA((3, n_hg)),
        ],
        compiler_params=pltpu.CompilerParams(
            collective_id=0, has_side_effects=True, vmem_limit_bytes=60 * 1024 * 1024
        ),
    )(block_mask, q.reshape(rows, latent), qr.transpose(1, 2, 0), kn, kr.T, g.reshape(rows, latent))
    made = (dq, dqr, dkn, dkr)
    dq, dqr, dkn, dkr = pl.pallas_call(
        hand_over,
        out_shape=tuple(jax.ShapeDtypeStruct(a.shape, a.dtype) for a in made),
        in_specs=[hbm] * 4,
        out_specs=[hbm] * 4,
        scratch_shapes=[pltpu.VMEM(a.shape, a.dtype) for a in made]
        + [pltpu.SemaphoreType.DMA((7,)), pltpu.SemaphoreType.DMA((7,))],
        compiler_params=pltpu.CompilerParams(vmem_limit_bytes=60 * 1024 * 1024),
    )(*made)
    return dq.reshape(tokens, heads, latent), dqr.transpose(2, 0, 1), dkn, dkr


def solution(mesh):
    wide = P("ctx", "hg", None)
    owned = P(("ctx", "hg"), None)
    return jax.shard_map(
        functools.partial(on_device, mesh.shape["ctx"], mesh.shape["hg"]),
        mesh=mesh,
        in_specs=(wide, wide, P("ctx", None), P("ctx", None), wide, P()),
        out_specs=(wide, wide, owned, owned),
        check_vma=False,
    )
```

```python
import functools
import math

import jax
import jax.numpy as jnp
from jax import lax
from jax.experimental import pallas as pl
from jax.experimental.pallas import tpu as pltpu
from jax.sharding import PartitionSpec as P

WINDOW = 4
PHASES = ((0, 1), (1, 1), (2, 2))
ORDER = (0, 2, 1, 3)
SCORE_SCALE = 192.0 ** (-0.5)
LOG2E = math.log2(math.e)
LANES = 128
MESH = pl.DeviceIdType.MESH


def dot_nn(a, b):
    return jnp.dot(a, b, preferred_element_type=jnp.float32)


def dot_nt(a, b):
    return lax.dot_general(a, b, (((1,), (1,)), ((), ())), preferred_element_type=jnp.float32)


def dot_tn(a, b):
    return lax.dot_general(a, b, (((0,), (0,)), ((), ())), preferred_element_type=jnp.float32)


def kernel(
    n_ctx,
    n_hg,
    mask_ref,
    q_hbm,
    qr_hbm,
    kn_hbm,
    kr_hbm,
    g_hbm,
    dq_ref,
    dqr_ref,
    dkn_ref,
    dkr_ref,
    q_ref,
    qrt_ref,
    qr_wide,
    qr_ref,
    g_ref,
    kn_all,
    krt_all,
    kr_all,
    dq_tile,
    dqr_wide,
    dqrt_ref,
    x_ref,
    dp_ref,
    prob_ref,
    ds_ref,
    top_ref,
    acc_ref,
    comb_out,
    comb_in,
    dk_out,
    dk_in,
    load_sem,
    store_sem,
    k_send,
    k_recv,
    c_sem,
    d_send,
    d_recv,
):
    rows, latent = q_ref.shape
    rope = qr_ref.shape[1]
    heads = qrt_ref.shape[0]
    tokens = qrt_ref.shape[2]
    keys = kn_all.shape[1]
    piece = keys // n_hg
    blocks = mask_ref.shape[0] // n_ctx
    block_rows = rows // blocks
    tile = 512
    tiles = rows // tile
    group = 256
    chunk = keys // blocks
    c = lax.axis_index("ctx")
    h = lax.axis_index("hg")

    load_kn = pltpu.make_async_copy(kn_hbm, kn_all.at[0], load_sem.at[0])
    load_kr = pltpu.make_async_copy(kr_hbm, krt_all.at[0], load_sem.at[1])
    load_q = pltpu.make_async_copy(q_hbm, q_ref, load_sem.at[2])
    load_qr = pltpu.make_async_copy(qr_hbm, qrt_ref, load_sem.at[3])
    load_g = pltpu.make_async_copy(g_hbm, g_ref, load_sem.at[4])
    load_kn.start()
    load_kr.start()

    core = lax.rem(c, 2)
    sibling = c + 1 - 2 * core
    ahead = lax.rem(c + 2, n_ctx)
    behind = lax.rem(c + n_ctx - 2, n_ctx)
    far = lax.rem(c + n_ctx - 3 + 6 * core, n_ctx)

    barrier = pltpu.get_barrier_semaphore()
    greeted = 0
    for where in (c, sibling, ahead, behind, far):
        for k in range(n_hg):
            if where is c and k == 0:
                continue
            pl.semaphore_signal(
                barrier,
                inc=1,
                device_id=(where, lax.rem(h + k, n_hg)),
                device_id_type=MESH,
            )
            greeted += 1
    load_q.start()
    load_qr.start()
    load_g.start()

    load_kn.wait()
    load_kr.wait()
    pl.semaphore_wait(barrier, greeted)

    def latent_copy(source, place, target, kind):
        return [
            pltpu.make_async_remote_copy(
                src_ref=buffer.at[source],
                dst_ref=buffer.at[place],
                send_sem=k_send.at[kind, part],
                recv_sem=k_recv.at[place, part],
                device_id=(target, h),
                device_id_type=MESH,
            )
            for part, buffer in enumerate((kn_all, krt_all))
        ]

    to_ahead = latent_copy(0, 1, ahead, 0)
    to_other = latent_copy(0, 2 + core, lax.rem(c + 1 + 2 * core, n_ctx), 1)
    handed_on = latent_copy(1, 3 - core, sibling, 2)
    for copy in to_ahead + to_other:
        copy.start()

    def wait_latents(place):
        for copy in latent_copy(0, place, sibling, 0):
            copy.wait_recv()

    bias = []
    for rb in range(blocks):
        for place, d in enumerate(ORDER):
            source = lax.rem(c - d + n_ctx, n_ctx)
            for kb in range(blocks):
                bit = mask_ref[c * blocks + rb, source * blocks + kb]
                bias.append(jnp.where(bit == 1, 0.0, -jnp.inf).astype(jnp.float32))

    acc_ref[...] = jnp.zeros_like(acc_ref)
    load_qr.wait()
    for head in range(heads):
        turned = qrt_ref[head].astype(jnp.float32).T
        qr_wide[pl.ds(head, tokens, stride=heads), :] = turned
    qr_ref[...] = qr_wide[...].astype(qr_ref.dtype)
    load_q.wait()
    load_g.wait()

    def turn_rope(place):
        kr_all[place] = krt_all[place].astype(jnp.float32).T.astype(kr_all.dtype)

    turn_rope(0)
    for phase, (first, count) in enumerate(PHASES):
        for place in range(first, first + count):
            if place == 0:
                continue
            wait_latents(place)
            if place == 1:
                for copy in handed_on:
                    copy.start()
            turn_rope(place)
        here = count * keys
        kn = kn_all[first : first + count].reshape(here, latent)
        kr = kr_all[first : first + count].reshape(here, rope)
        for i in range(tiles):
            r = slice(i * tile, (i + 1) * tile)
            rb = i * tile // block_rows
            s = dot_nt(kn, q_ref[r, :]) + dot_nt(kr, qr_ref[r, :])
            top = None
            for j in range(here // chunk):
                number = (rb * WINDOW + first) * blocks + j
                x = s[j * chunk : (j + 1) * chunk, :] * (SCORE_SCALE * LOG2E) + bias[number]
                x_ref[first * keys + j * chunk : first * keys + (j + 1) * chunk, r] = x
                part = jnp.max(x.reshape(chunk // 8, 8, tile), axis=0)
                top = part if top is None else jnp.maximum(top, part)
            top_ref[8 * phase : 8 * phase + 8, r] = top
            dp_ref[first * keys : first * keys + here, r] = dot_nt(kn, g_ref[r, :])

    def add_key_grads(first, count, r):
        mine = slice(first * keys, (first + count) * keys)
        ds = ds_ref[mine, r]
        acc_ref[mine, :latent] += dot_nn(ds, q_ref[r, :]) + dot_nn(prob_ref[mine, r], g_ref[r, :])
        acc_ref[mine, latent : latent + rope] += dot_nn(ds, qr_ref[r, :])

    def send_pieces(kind, target):
        out = []
        for k in reversed(range(n_hg)):
            if kind == 0 and k == 0:
                continue
            peer = lax.rem(h + k, n_hg)
            copy = pltpu.make_async_remote_copy(
                src_ref=dk_out.at[kind, peer],
                dst_ref=dk_in.at[kind, k],
                send_sem=d_send.at[kind, k],
                recv_sem=d_recv.at[kind, k],
                device_id=(target, peer),
                device_id_type=MESH,
            )
            copy.start()
            out.append((kind, k, copy))
        return out

    def split(block):
        return block.reshape(n_hg, piece, block.shape[1]).astype(dk_out.dtype)

    def one_of_last(which):
        return acc_ref[pl.ds(pl.multiple_of((2 + which) * keys, keys), keys), :]

    def folded(a):
        return jnp.sum(a.reshape(a.shape[0] // 8, 8, a.shape[1]), axis=0)

    for start in range(0, rows, tile):
        for at in range(start, start + tile, group):
            r = slice(at, at + group)
            top = jnp.max(top_ref[:, r], axis=0, keepdims=True)
            total = jnp.zeros((8, group), jnp.float32)
            mixed = jnp.zeros((8, group), jnp.float32)
            for k in range(0, WINDOW * keys, chunk):
                e = jnp.exp2(x_ref[k : k + chunk, r] - top)
                x_ref[k : k + chunk, r] = e
                total += folded(e)
                mixed += folded(e * dp_ref[k : k + chunk, r])
            inv = 1.0 / jnp.sum(total, axis=0, keepdims=True)
            delta = jnp.sum(mixed, axis=0, keepdims=True) * inv
            scaled = inv * SCORE_SCALE
            for k in range(0, WINDOW * keys, chunk):
                e = x_ref[k : k + chunk, r]
                prob_ref[k : k + chunk, r] = (e * inv).astype(jnp.bfloat16)
                ds = (e * scaled) * (dp_ref[k : k + chunk, r] - delta)
                ds_ref[k : k + chunk, r] = ds.astype(jnp.bfloat16)
        add_key_grads(2, 2, slice(start, start + tile))
    comb_out[...] = one_of_last(core).astype(comb_out.dtype)
    combine = pltpu.make_async_remote_copy(
        src_ref=comb_out,
        dst_ref=comb_in,
        send_sem=c_sem.at[0],
        recv_sem=c_sem.at[1],
        device_id=(sibling, h),
        device_id_type=MESH,
    )
    combine.start()
    dk_out[2] = split(one_of_last(1 - core))
    moving = send_pieces(2, lax.rem(c + n_ctx - 3 + 2 * core, n_ctx))

    for start in range(0, rows, 2 * tile):
        add_key_grads(1, 1, slice(start, start + 2 * tile))
    combine.wait_recv()
    dk_out[1] = split(acc_ref[keys : 2 * keys, :] + comb_in[...].astype(jnp.float32))
    moving += send_pieces(1, behind)

    for start in range(0, rows, 2 * tile):
        add_key_grads(0, 1, slice(start, start + 2 * tile))
    dk_out[0] = split(acc_ref[:keys, :])
    moving += send_pieces(0, c)

    stores = []
    for i in range(tiles):
        r = slice(i * tile, (i + 1) * tile)
        ds = ds_ref[:, r]
        dq_tile[r, :] = dot_tn(ds, kn_all[...].reshape(WINDOW * keys, latent)).astype(dq_tile.dtype)
        dqr_wide[r, :] = dot_tn(ds, kr_all[...].reshape(WINDOW * keys, rope))
        copy = pltpu.make_async_copy(dq_tile.at[r, :], dq_ref.at[r, :], store_sem.at[i])
        copy.start()
        stores.append(copy)
    for head in range(heads):
        part = dqr_wide[pl.ds(head, tokens, stride=heads), :]
        dqrt_ref[head] = part.T.astype(dqrt_ref.dtype)
    copy = pltpu.make_async_copy(dqrt_ref, dqr_ref, store_sem.at[tiles])
    copy.start()
    stores.append(copy)

    total = acc_ref[pl.ds(pl.multiple_of(h * piece, piece), piece), :]
    for kind, k, copy in sorted(moving, key=lambda m: (-m[0], m[1])):
        copy.wait_recv()
        total = total + dk_in[kind, k].astype(jnp.float32)
    dkn_ref[...] = total[:, :latent]
    dkr_ref[...] = total[:, latent : latent + rope]

    for copy in to_ahead + to_other + handed_on + [combine]:
        copy.wait_send()
    for copy in stores:
        copy.wait()
    for _, _, copy in moving:
        copy.wait_send()


def hand_over(dq_in, dqr_in, dkn_in, dkr_in, dq_ref, dqr_ref, dkn_ref, dkr_ref, dq, dqr, dkn, dkr, load_sem, store_sem):
    parts = []
    rows = dq.shape[0]
    step = rows // 4
    for at in range(0, rows, step):
        r = pl.ds(at, step)
        parts.append((dq_in.at[r, :], dq.at[r, :], dq_ref.at[r, :]))
    parts += [(dqr_in, dqr, dqr_ref), (dkn_in, dkn, dkn_ref), (dkr_in, dkr, dkr_ref)]
    loads = [pltpu.make_async_copy(a, b, load_sem.at[i]) for i, (a, b, _) in enumerate(parts)]
    stores = [pltpu.make_async_copy(b, o, store_sem.at[i]) for i, (_, b, o) in enumerate(parts)]
    for load in loads:
        load.start()
    for load, store in zip(loads, stores):
        load.wait()
        store.start()
    for store in stores:
        store.wait()


def on_device(n_ctx, n_hg, q, qr, kn, kr, g, block_mask):
    tokens, heads, latent = q.shape
    rope = qr.shape[2]
    rows = tokens * heads
    width = -(-(latent + rope) // LANES) * LANES
    piece = tokens // n_hg
    blocks = block_mask.shape[0] // n_ctx
    bf16, f32 = jnp.bfloat16, jnp.float32
    hbm = pl.BlockSpec(memory_space=pl.ANY)
    vmem = pl.BlockSpec(memory_space=pltpu.VMEM)
    dq, dqr, dkn, dkr = pl.pallas_call(
        functools.partial(kernel, n_ctx, n_hg),
        out_shape=(
            jax.ShapeDtypeStruct((rows, latent), bf16),
            jax.ShapeDtypeStruct((heads, rope, tokens), bf16),
            jax.ShapeDtypeStruct((piece, latent), f32),
            jax.ShapeDtypeStruct((piece, rope), f32),
        ),
        in_specs=[pl.BlockSpec(memory_space=pltpu.SMEM)] + [hbm] * 5,
        out_specs=[hbm, hbm, vmem, vmem],
        scratch_shapes=[
            pltpu.VMEM((rows, latent), bf16),
            pltpu.VMEM((heads, rope, tokens), bf16),
            pltpu.VMEM((rows, rope), f32),
            pltpu.VMEM((rows, rope), bf16),
            pltpu.VMEM((rows, latent), bf16),
            pltpu.VMEM((WINDOW, tokens, latent), bf16),
            pltpu.VMEM((WINDOW, rope, tokens), bf16),
            pltpu.VMEM((WINDOW, tokens, rope), bf16),
            pltpu.VMEM((rows, latent), bf16),
            pltpu.VMEM((rows, rope), f32),
            pltpu.VMEM((heads, rope, tokens), bf16),
            pltpu.VMEM((WINDOW * tokens, rows), f32),
            pltpu.VMEM((WINDOW * tokens, rows), f32),
            pltpu.VMEM((WINDOW * tokens, rows), bf16),
            pltpu.VMEM((WINDOW * tokens, rows), bf16),
            pltpu.VMEM((8 * len(PHASES), rows), f32),
            pltpu.VMEM((WINDOW * tokens, width), f32),
            pltpu.VMEM((tokens, width), bf16),
            pltpu.VMEM((tokens, width), bf16),
            pltpu.VMEM((3, n_hg, piece, width), bf16),
            pltpu.VMEM((3, n_hg, piece, width), bf16),
            pltpu.SemaphoreType.DMA((5,)),
            pltpu.SemaphoreType.DMA((rows // 512 + 1,)),
            pltpu.SemaphoreType.DMA((WINDOW, 2)),
            pltpu.SemaphoreType.DMA((WINDOW, 2)),
            pltpu.SemaphoreType.DMA((2,)),
            pltpu.SemaphoreType.DMA((3, n_hg)),
            pltpu.SemaphoreType.DMA((3, n_hg)),
        ],
        compiler_params=pltpu.CompilerParams(
            collective_id=0, has_side_effects=True, vmem_limit_bytes=60 * 1024 * 1024
        ),
    )(block_mask, q.reshape(rows, latent), qr.transpose(1, 2, 0), kn, kr.T, g.reshape(rows, latent))
    made = (dq, dqr, dkn, dkr)
    dq, dqr, dkn, dkr = pl.pallas_call(
        hand_over,
        out_shape=tuple(jax.ShapeDtypeStruct(a.shape, a.dtype) for a in made),
        in_specs=[hbm] * 4,
        out_specs=[hbm] * 4,
        scratch_shapes=[pltpu.VMEM(a.shape, a.dtype) for a in made]
        + [pltpu.SemaphoreType.DMA((7,)), pltpu.SemaphoreType.DMA((7,))],
        compiler_params=pltpu.CompilerParams(vmem_limit_bytes=60 * 1024 * 1024),
    )(*made)
    return dq.reshape(tokens, heads, latent), dqr.transpose(2, 0, 1), dkn, dkr


def solution(mesh):
    wide = P("ctx", "hg", None)
    owned = P(("ctx", "hg"), None)
    return jax.shard_map(
        functools.partial(on_device, mesh.shape["ctx"], mesh.shape["hg"]),
        mesh=mesh,
        in_specs=(wide, wide, P("ctx", None), P("ctx", None), wide, P()),
        out_specs=(wide, wide, owned, owned),
        check_vma=False,
    )
```
